256 devices in a mesh: ctx: 64 (over y_hi, z, x), head: 4 (over y_lo, core).
Axes of the slice: x: 4, y: 4 (y_hi: 2, y_lo: 2; y = y_hi * 2 + y_lo), z: 8, core: 2. Of those that a mesh axis runs over, the one named last changes fastest.
Arguments:
- qkv: bfloat16 [32768, 12288], P(('ctx', 'head')), may hold values from -26 to 26
- grad_out: bfloat16 [32768, 4096], P(('ctx', 'head')), may hold values from -6 to 6
- key_lists: int32 [256, 4], P('ctx'), may hold values from 0 to 255, as said below
- live_counts: int32 [256], P('ctx'), may hold values from 1 to 4
Outputs:
- grad_qkv: bfloat16 [32768, 12288], P(('ctx', 'head'))
The draws below stay inside these ranges and needn't reach their ends.
Inputs may be any that keep to these rules, and one draw needn't show every extreme that they name: `key_lists`: each entry names a block whose index of ctx is within 2 of its query block's and which is not within one block of its query block; the 4 entries of a row differ. Over all 4 entries of all rows (live or not) of one index of ctx, the blocks named on any other index of ctx are at most 2 of its blocks, and this is reached.
All inputs are finite; a program needn't handle non-finite values.
Results may differ from the reference program's by a relative error of at most 0.008.
Values may be sent and summed in bfloat16 or wider, within the bound.
No kernel may reach another device: no remote copies, remote signals or barrier semaphores. Data moves between devices by JAX's collectives and lax.ppermute only.
A program may use at most 192 MiB of HBM per device.

```python
import jax
import jax.numpy as jnp
from jax import lax

HEADS = 32
HD = 128
BLK = 128
SEARCHER_TILES = 4
DRAWN_TARGET_SET = 4
SPAN = 2
NAMED_TILE_LIMIT = 2
NB = 256
TOKENS = 32768


def draw_qkv(key, part):
    shape = (TOKENS, HEADS, 3, HD)
    base = jnp.clip(jax.random.normal(key, shape, jnp.float32), -6.0, 6.0)
    return base.reshape(TOKENS, HEADS * 3 * HD).astype(jnp.bfloat16)


def draw_key_lists(key, part):
    shard_total = NB // SEARCHER_TILES
    neighbourhood_halfwidth = 2 * SPAN
    sides = jnp.array([side for side in range(-SPAN, SPAN + 1) if side != 0], dtype=jnp.int32)

    def pick_allowed(subkey):
        return jax.random.permutation(subkey, SEARCHER_TILES)[:NAMED_TILE_LIMIT].astype(jnp.int32)
    allowed = jax.vmap(pick_allowed)(jax.random.split(jax.random.fold_in(key, 11), shard_total * neighbourhood_halfwidth))
    allowed = allowed.reshape(shard_total, neighbourhood_halfwidth, NAMED_TILE_LIMIT)
    tile_ordinals = jnp.arange(NB, dtype=jnp.int32)
    shard_of = tile_ordinals // SEARCHER_TILES
    own_blocks = shard_of[:, None] * SEARCHER_TILES + jnp.arange(SEARCHER_TILES, dtype=jnp.int32)[None, :]
    neighbour = shard_of[:, None] + sides[None, :]
    picked = allowed[shard_of]
    far_blocks = (neighbour[:, :, None] * SEARCHER_TILES + picked).reshape(NB, neighbourhood_halfwidth * NAMED_TILE_LIMIT)
    far_ok = jnp.repeat((neighbour >= 0) & (neighbour < shard_total), NAMED_TILE_LIMIT, axis=1)
    candidates = jnp.concatenate([own_blocks, far_blocks], axis=1)
    usable = jnp.concatenate([jnp.ones((NB, SEARCHER_TILES), bool), far_ok], axis=1)
    usable = usable & (jnp.abs(candidates - tile_ordinals[:, None]) > 1)
    width_all = SEARCHER_TILES + neighbourhood_halfwidth * NAMED_TILE_LIMIT

    def row_order(subkey):
        return jax.random.permutation(subkey, width_all).astype(jnp.int32)
    orders = jax.vmap(row_order)(jax.random.split(jax.random.fold_in(key, 13), NB)) + 1
    tile_merits = jnp.where(usable, orders, 0)
    target_positions = jnp.arange(width_all, dtype=jnp.int32)
    preference_reward = jnp.where((tile_ordinals[:, None] == 0) & (target_positions[None, :] >= SEARCHER_TILES + (neighbourhood_halfwidth - 1) * NAMED_TILE_LIMIT), 1000, 0)
    sorted_tiles = lax.top_k(tile_merits + preference_reward, DRAWN_TARGET_SET)[1]
    return jnp.take_along_axis(candidates, sorted_tiles, axis=1).astype(jnp.int32)


def touch_ends(values, key, low, top_value):
    longest = values.shape.index(max(values.shape))
    spots = []
    for shift in (0, 1):
        where = [jax.random.randint(jax.random.fold_in(key, axis), (), 0, length) for axis, length in enumerate(values.shape)]
        where[longest] = (where[longest] + shift) % values.shape[longest]
        spots.append(tuple(where))
    return values.at[spots[0]].set(low).at[spots[1]].set(top_value)


def block_scale(own_key, dims, cuts, smallest, high):
    gain, own = 1.0, jax.random.fold_in(own_key, 6)
    for position, parts in cuts:
        steps = jnp.exp(jax.random.uniform(jax.random.fold_in(own, position), (parts,), jnp.float32, smallest / len(cuts), high / len(cuts)))
        gain = gain * jnp.repeat(steps, dims[position] // parts).reshape([-1 if axis == position else 1 for axis in range(len(dims))])
    return gain


def noise(key, dims, scale, reach, cuts=(), held_as=jnp.bfloat16):
    values = jax.random.normal(key, dims, jnp.float32) * scale
    if len(cuts) > 0:
        values = block_scale(key, dims, cuts, -0.22, 0.18) * values
    return jnp.clip(values, min=-reach, max=reach).astype(held_as)


def setup_inputs(seed: int = 0) -> dict:
    arg_keys = jax.random.split(jax.random.key(seed), 5)
    qkv = draw_qkv(jax.random.fold_in(arg_keys[4], 71), 0)
    grad_out = noise(arg_keys[1], (TOKENS, HEADS * HD), 1.0, 6.0, ((0, 256),))
    key_lists = draw_key_lists(jax.random.fold_in(arg_keys[4], 71), 0)
    live_counts = touch_ends(jax.random.randint(arg_keys[3], (NB,), 1, DRAWN_TARGET_SET + 1), jax.random.fold_in(arg_keys[3], 1), 1, DRAWN_TARGET_SET).astype(jnp.int32)
    return {"qkv": qkv, "grad_out": grad_out, "key_lists": key_lists, "live_counts": live_counts}


def reference(qkv, grad_out, key_lists, live_counts):
    total_blocks = key_lists.shape[0]
    scaling = HD ** -0.5
    merged = qkv.reshape(total_blocks, BLK, HEADS, 3, HD)
    queries = merged[:, :, :, 0]
    key_rows = merged[:, :, :, 1]
    value_rows = merged[:, :, :, 2]
    grads_in = grad_out.reshape(total_blocks, BLK, HEADS, HD)

    def one_block(totals, block_id):
        window = block_id - 1 + jnp.arange(3, dtype=jnp.int32)
        listed = key_lists[block_id].astype(jnp.int32)
        named = jnp.concatenate([window, listed]).astype(jnp.int32)
        usable = jnp.concatenate([(window >= 0) & (window < total_blocks), jnp.arange(DRAWN_TARGET_SET, dtype=jnp.int32) < live_counts[block_id]])
        clipped = jnp.clip(named, 0, total_blocks - 1).astype(jnp.int32)
        key_part = key_rows[clipped].astype(jnp.float32)
        value_part = value_rows[clipped].astype(jnp.float32)
        query_part = queries[block_id].astype(jnp.float32)
        grad_part = grads_in[block_id].astype(jnp.float32)
        weight = usable.astype(jnp.float32)[None, None, :, None]
        tile_merits = jnp.einsum("qhd,nkhd->hqnk", query_part, key_part) * scaling
        masked = jnp.where(weight > 0.0, tile_merits, -1.0e30)
        highest = jnp.max(masked, axis=(2, 3), keepdims=True)
        powers = jnp.exp(masked - highest) * weight
        soft_weights = powers / jnp.sum(powers, axis=(2, 3), keepdims=True)
        grad_soft = jnp.einsum("qhd,nkhd->hqnk", grad_part, value_part)
        row_delta = jnp.sum(soft_weights * grad_soft, axis=(2, 3), keepdims=True)
        grad_scores = soft_weights * (grad_soft - row_delta)
        soft_low = soft_weights.astype(jnp.bfloat16).astype(jnp.float32)
        scores_low = grad_scores.astype(jnp.bfloat16).astype(jnp.float32)
        grad_values = jnp.einsum("hqnk,qhd->nkhd", soft_low, grad_part)
        grad_keys = jnp.einsum("hqnk,qhd->nkhd", scores_low, query_part) * scaling
        grad_query = jnp.einsum("hqnk,nkhd->qhd", scores_low, key_part) * scaling
        totals = totals.at[clipped].add(jnp.stack([grad_keys, grad_values], axis=3))
        return totals, grad_query

    start_totals = jnp.zeros((total_blocks, BLK, HEADS, 2, HD), jnp.float32)
    totals, grad_query = lax.scan(one_block, start_totals, jnp.arange(total_blocks, dtype=jnp.int32))
    joined = jnp.concatenate([grad_query[:, :, :, None, :], totals], axis=3)
    return joined.astype(jnp.bfloat16).reshape(total_blocks * BLK, HEADS * 3 * HD)
```

```python
import functools

import jax
import jax.numpy as jnp
from jax import lax
from jax.experimental import pallas as pl
from jax.experimental.pallas import tpu as pltpu
from jax.sharding import Mesh
from jax.sharding import PartitionSpec as P

HD = 128
BLK = 128
TILES = 4
SPAN = 2
LISTED = 4
WIN = 3
RING = 4
GROUP = RING * TILES
HALO = SPAN * TILES
EXT = GROUP + 2 * HALO
LOCAL = 2
SLOTS = WIN + LISTED
COLS = LOCAL * 3 * HD
LOG2E = 1.4426950408889634
F32 = jnp.float32
BF16 = jnp.bfloat16


PAIR = 2


def send_kernel(flip_ref, qkv_ref, grad_ref, kv_ref, qd_ref):
    for part in range(PAIR):
        for h in range(LOCAL):
            at = (part * LOCAL + h) * 3 * HD
            gat = (part * LOCAL + h) * HD
            kv_ref[part, h] = qkv_ref[:, at + HD : at + 3 * HD]
            qd_ref[part, h, :, 0:HD] = qkv_ref[:, at : at + HD]
            qd_ref[part, h, :, HD : 2 * HD] = grad_ref[:, gat : gat + HD]


def split_heads(flip, qkv, grad_out):
    def there(g, flip_ref):
        return (jnp.bitwise_xor(g, flip_ref[0]), 0, 0, 0)

    parts = jax.ShapeDtypeStruct((GROUP, LOCAL, BLK, 2 * HD), BF16)
    return pl.pallas_call(
        send_kernel,
        out_shape=[parts, parts],
        grid_spec=pltpu.PrefetchScalarGridSpec(
            num_scalar_prefetch=1,
            grid=(GROUP // PAIR,),
            in_specs=[
                pl.BlockSpec((BLK, PAIR * COLS), lambda g, f: (0, g)),
                pl.BlockSpec((BLK, PAIR * LOCAL * HD), lambda g, f: (0, g)),
            ],
            out_specs=[
                pl.BlockSpec((PAIR, LOCAL, BLK, 2 * HD), there),
                pl.BlockSpec((PAIR, LOCAL, BLK, 2 * HD), there),
            ],
        ),
        cost_estimate=pl.CostEstimate(flops=0, bytes_accessed=8 << 20, transcendentals=0),
    )(flip, qkv, grad_out)


def join_kernel(flip_ref, dq_ref, dkv_ref, out_ref):
    for part in range(PAIR):
        for h in range(LOCAL):
            at = (part * LOCAL + h) * 3 * HD
            out_ref[:, at : at + HD] = dq_ref[part, h]
            out_ref[:, at + HD : at + 3 * HD] = dkv_ref[part, h]


def join_heads(flip, dq, dkv):
    def there(g, flip_ref):
        return (jnp.bitwise_xor(g, flip_ref[0]), 0, 0, 0)

    return pl.pallas_call(
        join_kernel,
        out_shape=jax.ShapeDtypeStruct((BLK, GROUP * COLS), BF16),
        grid_spec=pltpu.PrefetchScalarGridSpec(
            num_scalar_prefetch=1,
            grid=(GROUP // PAIR,),
            in_specs=[
                pl.BlockSpec((PAIR, LOCAL, BLK, HD), there),
                pl.BlockSpec((PAIR, LOCAL, BLK, 2 * HD), there),
            ],
            out_specs=pl.BlockSpec((BLK, PAIR * COLS), lambda g, f: (0, g)),
        ),
        cost_estimate=pl.CostEstimate(flops=0, bytes_accessed=6 << 20, transcendentals=0),
    )(flip, dq, dkv)


def attention_kernel(
    head,
    place_ref,
    live_ref,
    kv_ref,
    before_ref,
    after_ref,
    qd_ref,
    dq_ref,
    own_ref,
    tobefore_ref,
    toafter_ref,
    kv,
    qd,
    acc,
    mix,
    tall,
    low,
    dqs,
    outs,
    sem,
):
    loads = [
        pltpu.make_async_copy(before_ref.at[:, head], kv.at[pl.ds(0, HALO)], sem.at[0]),
        pltpu.make_async_copy(kv_ref.at[:, head], kv.at[pl.ds(HALO, GROUP)], sem.at[1]),
        pltpu.make_async_copy(after_ref.at[:, head], kv.at[pl.ds(HALO + GROUP, HALO)], sem.at[2]),
        pltpu.make_async_copy(qd_ref.at[:, head], qd, sem.at[3]),
    ]
    for c in loads:
        c.start()
    acc[...] = jnp.zeros_like(acc)
    mix[...] = jnp.zeros_like(mix)
    for c in loads:
        c.wait()
    scale = HD ** (-0.5)

    def one_block(block, _):
        mix[0:BLK, 0:HD] = qd[block, :, 0:HD]
        mix[BLK : 2 * BLK, HD : 2 * HD] = qd[block, :, HD : 2 * HD]
        weights = mix[...]
        high = jnp.full((8, BLK), -3e38, F32)
        for j in range(SLOTS):
            place = place_ref[block, j]
            both = lax.dot_general(
                kv[place], weights, (((1,), (1,)), ((), ())), preferred_element_type=F32
            )
            bias = jnp.where(live_ref[block, j] > 0, 0.0, -1e30).astype(F32)
            scores = both[:, 0:BLK] * (scale * LOG2E) + bias
            tall[j, :, 0:BLK] = scores
            tall[j, :, BLK : 2 * BLK] = both[:, BLK : 2 * BLK]
            high = jnp.maximum(high, jnp.max(scores.reshape(BLK // 8, 8, BLK), axis=0))
        top = jnp.max(high, axis=0, keepdims=True)
        total = jnp.zeros((8, BLK), F32)
        cross = jnp.zeros((8, BLK), F32)
        for j in range(SLOTS):
            powers = jnp.exp2(tall[j, :, 0:BLK] - top)
            tall[j, :, 0:BLK] = powers
            total = total + jnp.sum(powers.reshape(BLK // 8, 8, BLK), axis=0)
            cross = cross + jnp.sum(
                (powers * tall[j, :, BLK : 2 * BLK]).reshape(BLK // 8, 8, BLK), axis=0
            )
        inverse = 1.0 / jnp.sum(total, axis=0, keepdims=True)
        delta = jnp.sum(cross, axis=0, keepdims=True) * inverse
        grad_query = jnp.zeros((BLK, HD), F32)
        for j in range(SLOTS):
            place = place_ref[block, j]
            soft = tall[j, :, 0:BLK] * inverse
            grads = (soft * (tall[j, :, BLK : 2 * BLK] - delta)).astype(BF16)
            low[j, :, 0:BLK] = grads
            low[j, :, BLK : 2 * BLK] = soft.astype(BF16)
            grad_query = grad_query + lax.dot_general(
                grads, kv[place, :, 0:HD], (((0,), (0,)), ((), ())), preferred_element_type=F32
            )
            acc[place] += lax.dot_general(
                low[j], weights, (((1,), (0,)), ((), ())), preferred_element_type=F32
            )
        dqs[block] = (grad_query * scale).astype(BF16)
        return 0

    lax.fori_loop(0, GROUP, one_block, 0)

    def finish(place, _):
        acc[place, :, 0:HD] = acc[place, :, 0:HD] * scale
        return 0

    lax.fori_loop(0, EXT, finish, 0)
    outs[0:HALO] = acc[0:HALO].astype(BF16)
    outs[HALO : 2 * HALO] = acc[HALO + GROUP : EXT].astype(BF16)
    stores = [
        pltpu.make_async_copy(dqs, dq_ref, sem.at[0]),
        pltpu.make_async_copy(acc.at[pl.ds(HALO, GROUP)], own_ref, sem.at[1]),
        pltpu.make_async_copy(outs.at[pl.ds(0, HALO)], tobefore_ref, sem.at[2]),
        pltpu.make_async_copy(outs.at[pl.ds(HALO, HALO)], toafter_ref, sem.at[3]),
    ]
    for c in stores:
        c.start()
    for c in stores:
        c.wait()


def attention(head, places, live, kv, before, after, qd):
    hbm = pl.BlockSpec(memory_space=pl.ANY)
    smem = pl.BlockSpec(memory_space=pltpu.SMEM)
    return pl.pallas_call(
        functools.partial(attention_kernel, head),
        out_shape=[
            jax.ShapeDtypeStruct((GROUP, BLK, HD), BF16),
            jax.ShapeDtypeStruct((GROUP, BLK, 2 * HD), F32),
            jax.ShapeDtypeStruct((HALO, BLK, 2 * HD), BF16),
            jax.ShapeDtypeStruct((HALO, BLK, 2 * HD), BF16),
        ],
        in_specs=[smem, smem, hbm, hbm, hbm, hbm],
        out_specs=[hbm, hbm, hbm, hbm],
        scratch_shapes=[
            pltpu.VMEM((EXT, BLK, 2 * HD), BF16),
            pltpu.VMEM((GROUP, BLK, 2 * HD), BF16),
            pltpu.VMEM((EXT, BLK, 2 * HD), F32),
            pltpu.VMEM((2 * BLK, 2 * HD), BF16),
            pltpu.VMEM((SLOTS, BLK, 2 * BLK), F32),
            pltpu.VMEM((SLOTS, BLK, 2 * BLK), BF16),
            pltpu.VMEM((GROUP, BLK, HD), BF16),
            pltpu.VMEM((2 * HALO, BLK, 2 * HD), BF16),
            pltpu.SemaphoreType.DMA((4,)),
        ],
        compiler_params=pltpu.CompilerParams(vmem_limit_bytes=32 << 20),
        cost_estimate=pl.CostEstimate(
            flops=2_400_000_000, bytes_accessed=8 << 20, transcendentals=2_000_000
        ),
    )(places, live, kv, before, after, qd)


def shards(qkv, grad_out, key_lists, live_counts):
    planes = lax.axis_size("zz")
    plane = lax.axis_index("zz")
    team = ("x", "head")
    half = planes // 2
    flip = jnp.where(plane >= half, 1, 0).astype(jnp.int32).reshape(1)

    def crossing(step):
        pairs = []
        for p in range(planes):
            q = p + step
            if 0 <= q < planes:
                for r in range(RING):
                    for h in range(4):
                        other = h ^ 2 if (p >= half) != (q >= half) else h
                        pairs.append(((p * RING + r) * 4 + h, (q * RING + r) * 4 + other))
        return pairs

    everyone = ("zz", "x", "head")
    to_next = functools.partial(lax.ppermute, axis_name=everyone, perm=crossing(1))
    to_prev = functools.partial(lax.ppermute, axis_name=everyone, perm=crossing(-1))

    named = jnp.concatenate([key_lists, live_counts[:, None]], axis=1)
    ring = [named]
    for step in range(1, RING):
        ring.append(lax.ppermute(named, "x", [(i, (i + step) % RING) for i in range(RING)]))
    behind = jnp.mod(lax.axis_index("x") - jnp.arange(RING, dtype=jnp.int32), RING)
    named = jnp.take(jnp.stack(ring), behind, axis=0).reshape(GROUP, LISTED + 1)
    blocks = plane * GROUP + jnp.arange(GROUP, dtype=jnp.int32)
    window = blocks[:, None] - 1 + jnp.arange(WIN, dtype=jnp.int32)[None, :]
    window_ok = (window >= 0) & (window < planes * GROUP)
    listed_ok = jnp.arange(LISTED, dtype=jnp.int32)[None, :] < named[:, LISTED:]
    live = jnp.concatenate([window_ok, listed_ok], axis=1).astype(jnp.int32)
    places = jnp.concatenate([window, named[:, :LISTED]], axis=1) - plane * GROUP + HALO

    kv, qd = split_heads(flip, qkv, grad_out)
    kv = lax.all_to_all(kv, team, 0, 0, tiled=True)
    qd = lax.all_to_all(qd, team, 0, 0, tiled=True)
    before = to_next(kv[GROUP - HALO :])
    after = to_prev(kv[:HALO])

    dqs, dkvs = [], []
    for h in range(LOCAL):
        dq, own, tobefore, toafter = attention(h, places, live, kv, before, after, qd)
        from_next = to_prev(tobefore)
        from_prev = to_next(toafter)
        dkv = jnp.concatenate(
            [
                own[:HALO] + from_prev.astype(F32),
                own[HALO:] + from_next.astype(F32),
            ],
            axis=0,
        ).astype(BF16)
        dqs.append(dq)
        dkvs.append(dkv)
    dq = lax.all_to_all(jnp.stack(dqs, axis=1), team, 0, 0, tiled=True)
    dkv = lax.all_to_all(jnp.stack(dkvs, axis=1), team, 0, 0, tiled=True)
    return join_heads(flip, dq, dkv)


def solution(mesh):
    shape = mesh.devices.shape
    inner = Mesh(mesh.devices.reshape(shape[0] // RING, RING, shape[1]), ("zz", "x", "head"))
    everyone = ("zz", "x", "head")
    placed = (P(everyone, None), P(everyone, None), P(("zz", "x"), None), P(("zz", "x")))
    return jax.shard_map(
        shards, mesh=inner, in_specs=placed, out_specs=P(everyone, None), check_vma=False
    )
```

```python
import functools

import jax
import jax.numpy as jnp
from jax import lax
from jax.experimental import pallas as pl
from jax.experimental.pallas import tpu as pltpu
from jax.sharding import Mesh
from jax.sharding import PartitionSpec as P

HD = 128
BLK = 128
TILES = 4
SPAN = 2
LISTED = 4
WIN = 3
RING = 4
GROUP = RING * TILES
HALO = SPAN * TILES
EXT = GROUP + 2 * HALO
LOCAL = 2
SLOTS = WIN + LISTED
COLS = LOCAL * 3 * HD
LOG2E = 1.4426950408889634
F32 = jnp.float32
BF16 = jnp.bfloat16


VMEM = pl.BlockSpec(memory_space=pltpu.VMEM)
SMEM = pl.BlockSpec(memory_space=pltpu.SMEM)
HBM = pl.BlockSpec(memory_space=pl.ANY)


def run_all(pairs, sem):
    running = [pltpu.make_async_copy(s, d, sem.at[i]) for i, (s, d) in enumerate(pairs)]
    for c in running:
        c.start()
    for c in running:
        c.wait()


def columns(part, flip, head):
    pair = (part // 4) * 4 + jnp.bitwise_xor(part % 4, flip)
    at = pair * LOCAL + head
    return pl.multiple_of(at * 3 * HD, 3 * HD), pl.multiple_of(at * HD, HD)


def send_pairs_kernel(flip_ref, qkv_ref, kv_ref, sem):
    pairs = []
    for part in range(GROUP):
        for h in range(LOCAL):
            at, _ = columns(part, flip_ref[0], h)
            pairs.append((qkv_ref.at[:, pl.ds(at + HD, 2 * HD)], kv_ref.at[part, h]))
    run_all(pairs, sem)


def send_pairs(flip, qkv):
    return pl.pallas_call(
        send_pairs_kernel,
        out_shape=jax.ShapeDtypeStruct((GROUP, LOCAL, BLK, 2 * HD), BF16),
        in_specs=[SMEM, HBM],
        out_specs=VMEM,
        scratch_shapes=[pltpu.SemaphoreType.DMA((GROUP * LOCAL,))],
        compiler_params=pltpu.CompilerParams(vmem_limit_bytes=8 << 20),
        cost_estimate=pl.CostEstimate(flops=0, bytes_accessed=4 << 20, transcendentals=0),
    )(flip, qkv)


def send_queries_kernel(flip_ref, qkv_ref, grad_ref, qd0_ref, qd1_ref, sem):
    pairs = []
    for part in range(GROUP):
        for h, qd_ref in enumerate((qd0_ref, qd1_ref)):
            at, gat = columns(part, flip_ref[0], h)
            pairs.append((qkv_ref.at[:, pl.ds(at, HD)], qd_ref.at[part, :, pl.ds(0, HD)]))
            pairs.append((grad_ref.at[:, pl.ds(gat, HD)], qd_ref.at[part, :, pl.ds(HD, HD)]))
    run_all(pairs, sem)


def send_queries(flip, qkv, grad_out):
    part = jax.ShapeDtypeStruct((GROUP, BLK, 2 * HD), BF16)
    return pl.pallas_call(
        send_queries_kernel,
        out_shape=[part, part],
        in_specs=[SMEM, HBM, HBM],
        out_specs=[VMEM, VMEM],
        scratch_shapes=[pltpu.SemaphoreType.DMA((GROUP * LOCAL * 2,))],
        compiler_params=pltpu.CompilerParams(vmem_limit_bytes=8 << 20),
        cost_estimate=pl.CostEstimate(flops=0, bytes_accessed=4 << 20, transcendentals=0),
    )(flip, qkv, grad_out)


def join_early_kernel(flip_ref, dq0_ref, mid_ref, out_ref, sem):
    pairs = []
    for part in range(GROUP):
        at0, _ = columns(part, flip_ref[0], 0)
        at1, _ = columns(part, flip_ref[0], 1)
        pairs.append((dq0_ref.at[part], out_ref.at[:, pl.ds(at0, HD)]))
        pairs.append((mid_ref.at[part, :, pl.ds(0, HD)], out_ref.at[:, pl.ds(at1, HD)]))
        pairs.append(
            (mid_ref.at[part, :, pl.ds(HD, 2 * HD)], out_ref.at[:, pl.ds(at0 + HD, 2 * HD)])
        )
    run_all(pairs, sem)


def join_early(flip, dq0, mid):
    return pl.pallas_call(
        join_early_kernel,
        out_shape=jax.ShapeDtypeStruct((BLK, GROUP * COLS), BF16),
        in_specs=[SMEM, VMEM, VMEM],
        out_specs=HBM,
        scratch_shapes=[pltpu.SemaphoreType.DMA((GROUP * 3,))],
        compiler_params=pltpu.CompilerParams(vmem_limit_bytes=8 << 20),
        cost_estimate=pl.CostEstimate(flops=0, bytes_accessed=4 << 20, transcendentals=0),
    )(flip, dq0, mid)


def join_late_kernel(flip_ref, dkv_ref, held_ref, out_ref, sem):
    pairs = []
    for part in range(GROUP):
        at, _ = columns(part, flip_ref[0], 1)
        pairs.append((dkv_ref.at[part], out_ref.at[:, pl.ds(at + HD, 2 * HD)]))
    run_all(pairs, sem)


def join_late(flip, dkv, held):
    return pl.pallas_call(
        join_late_kernel,
        out_shape=jax.ShapeDtypeStruct((BLK, GROUP * COLS), BF16),
        in_specs=[SMEM, VMEM, HBM],
        out_specs=HBM,
        scratch_shapes=[pltpu.SemaphoreType.DMA((GROUP,))],
        input_output_aliases={2: 0},
        compiler_params=pltpu.CompilerParams(vmem_limit_bytes=8 << 20),
        cost_estimate=pl.CostEstimate(flops=0, bytes_accessed=2 << 20, transcendentals=0),
    )(flip, dkv, held)


def add_kernel(acc_ref, prev_ref, next_ref, *refs):
    out_ref = refs[-1]
    left = 0
    if len(refs) == 2:
        out_ref[:, :, 0:HD] = refs[0][...]
        left = HD
    for b in range(GROUP):
        more = prev_ref[b] if b < HALO else next_ref[b - HALO]
        sums = acc_ref[b]
        dk = sums[:, 0:HD] * (HD ** (-0.5)) + more[:, 0:HD].astype(F32)
        dv = sums[:, HD : 2 * HD] + more[:, HD : 2 * HD].astype(F32)
        out_ref[b, :, left : left + HD] = dk.astype(BF16)
        out_ref[b, :, left + HD : left + 2 * HD] = dv.astype(BF16)


def add_halo(acc, from_prev, from_next, *dq):
    width = (3 if dq else 2) * HD
    return pl.pallas_call(
        add_kernel,
        out_shape=jax.ShapeDtypeStruct((GROUP, BLK, width), BF16),
        in_specs=[VMEM] * (3 + len(dq)),
        out_specs=VMEM,
        compiler_params=pltpu.CompilerParams(vmem_limit_bytes=12 << 20),
        cost_estimate=pl.CostEstimate(flops=2 << 20, bytes_accessed=4 << 20, transcendentals=0),
    )(acc, from_prev, from_next, *dq)


def attention_kernel(
    head,
    place_ref,
    live_ref,
    kv_ref,
    before_ref,
    after_ref,
    qd,
    dq_ref,
    own_ref,
    tobefore_ref,
    toafter_ref,
    kv,
    acc,
    mix,
    chosen,
    tall,
    low,
    dqs,
    outs,
    sem,
):
    loads = [
        pltpu.make_async_copy(before_ref, kv.at[pl.ds(0, HALO)], sem.at[0]),
        pltpu.make_async_copy(kv_ref.at[:, head], kv.at[pl.ds(HALO, GROUP)], sem.at[1]),
        pltpu.make_async_copy(after_ref, kv.at[pl.ds(HALO + GROUP, HALO)], sem.at[2]),
    ]
    for c in loads:
        c.start()
    acc[...] = jnp.zeros_like(acc)
    mix[...] = jnp.zeros_like(mix)
    for c in loads:
        c.wait()
    scale = HD ** (-0.5)

    def begin(block, side):
        mix[side, 0:BLK, 0:HD] = qd[block, :, 0:HD]
        mix[side, BLK : 2 * BLK, HD : 2 * HD] = qd[block, :, HD : 2 * HD]
        for j in range(SLOTS):
            chosen[side, j * BLK : (j + 1) * BLK] = kv[place_ref[block, j]]
        tall[side] = lax.dot_general(
            chosen[side], mix[side], (((1,), (1,)), ((), ())), preferred_element_type=F32
        )

    def middle(block, side):
        high = jnp.full((8, BLK), -3e38, F32)
        biases = [jnp.where(live_ref[block, j] > 0, 0.0, -1e30).astype(F32) for j in range(SLOTS)]
        for j in range(SLOTS):
            scores = tall[side, j * BLK : (j + 1) * BLK, 0:BLK] * (scale * LOG2E) + biases[j]
            high = jnp.maximum(high, jnp.max(scores.reshape(BLK // 8, 8, BLK), axis=0))
        top = jnp.max(high, axis=0, keepdims=True)
        total = jnp.zeros((8, BLK), F32)
        cross = jnp.zeros((8, BLK), F32)
        for j in range(SLOTS):
            rows = slice(j * BLK, (j + 1) * BLK)
            powers = jnp.exp2(tall[side, rows, 0:BLK] * (scale * LOG2E) + (biases[j] - top))
            tall[side, rows, 0:BLK] = powers
            total = total + jnp.sum(powers.reshape(BLK // 8, 8, BLK), axis=0)
            cross = cross + jnp.sum(
                (powers * tall[side, rows, BLK : 2 * BLK]).reshape(BLK // 8, 8, BLK), axis=0
            )
        inverse = 1.0 / jnp.sum(total, axis=0, keepdims=True)
        delta = jnp.sum(cross, axis=0, keepdims=True) * inverse
        for j in range(SLOTS):
            rows = slice(j * BLK, (j + 1) * BLK)
            soft = tall[side, rows, 0:BLK] * inverse
            low[side, rows, 0:BLK] = (soft * (tall[side, rows, BLK : 2 * BLK] - delta)).astype(BF16)
            low[side, rows, BLK : 2 * BLK] = soft.astype(BF16)

    def end(block, side):
        grad_query = lax.dot_general(
            low[side, :, 0:BLK], chosen[side, :, 0:HD], (((0,), (0,)), ((), ())), preferred_element_type=F32
        )
        dqs[block] = (grad_query * scale).astype(BF16)
        back = lax.dot_general(
            low[side], mix[side], (((1,), (0,)), ((), ())), preferred_element_type=F32
        )
        for j in range(SLOTS):
            acc[place_ref[block, j]] += back[j * BLK : (j + 1) * BLK]

    def step(i, _):
        for k in range(4):
            begin(4 * i + k, k)
        for k in range(4):
            middle(4 * i + k, k)
        for k in range(4):
            end(4 * i + k, k)
        return 0

    lax.fori_loop(0, GROUP // 4, step, 0)

    column = lax.broadcasted_iota(jnp.int32, (1, 1, 2 * HD), 2)
    factor = jnp.where(column < HD, scale, 1.0).astype(F32)
    stores = [
        pltpu.make_async_copy(dqs, dq_ref, sem.at[0]),
        pltpu.make_async_copy(acc.at[pl.ds(HALO, GROUP)], own_ref, sem.at[1]),
        pltpu.make_async_copy(outs.at[pl.ds(0, HALO)], tobefore_ref, sem.at[2]),
        pltpu.make_async_copy(outs.at[pl.ds(HALO, HALO)], toafter_ref, sem.at[3]),
    ]
    for c in stores[:2]:
        c.start()
    outs[0:HALO] = (acc[0:HALO] * factor).astype(BF16)
    outs[HALO : 2 * HALO] = (acc[HALO + GROUP : EXT] * factor).astype(BF16)
    for c in stores[2:]:
        c.start()
    for c in stores:
        c.wait()


def attention(head, places, live, kv, before, after, qd):
    return pl.pallas_call(
        functools.partial(attention_kernel, head),
        out_shape=[
            jax.ShapeDtypeStruct((GROUP, BLK, HD), BF16),
            jax.ShapeDtypeStruct((GROUP, BLK, 2 * HD), F32),
            jax.ShapeDtypeStruct((HALO, BLK, 2 * HD), BF16),
            jax.ShapeDtypeStruct((HALO, BLK, 2 * HD), BF16),
        ],
        in_specs=[SMEM, SMEM, HBM, HBM, HBM, VMEM],
        out_specs=[HBM] * 4,
        scratch_shapes=[
            pltpu.VMEM((EXT, BLK, 2 * HD), BF16),
            pltpu.VMEM((EXT, BLK, 2 * HD), F32),
            pltpu.VMEM((4, 2 * BLK, 2 * HD), BF16),
            pltpu.VMEM((4, SLOTS * BLK, 2 * HD), BF16),
            pltpu.VMEM((4, SLOTS * BLK, 2 * BLK), F32),
            pltpu.VMEM((4, SLOTS * BLK, 2 * BLK), BF16),
            pltpu.VMEM((GROUP, BLK, HD), BF16),
            pltpu.VMEM((2 * HALO, BLK, 2 * HD), BF16),
            pltpu.SemaphoreType.DMA((4,)),
        ],
        compiler_params=pltpu.CompilerParams(vmem_limit_bytes=20 << 20),
        cost_estimate=pl.CostEstimate(
            flops=2_400_000_000, bytes_accessed=8 << 20, transcendentals=2_000_000
        ),
    )(places, live, kv, before, after, qd)


def shards(qkv, grad_out, key_lists, live_counts):
    planes = lax.axis_size("zz")
    plane = lax.axis_index("zz")
    team = ("x", "head")
    half = planes // 2
    flip = jnp.where(plane >= half, 2, 0).astype(jnp.int32).reshape(1)

    def crossing(step):
        pairs = []
        for p in range(planes):
            q = p + step
            if 0 <= q < planes:
                for r in range(RING):
                    for h in range(4):
                        other = h ^ 2 if (p >= half) != (q >= half) else h
                        pairs.append(((p * RING + r) * 4 + h, (q * RING + r) * 4 + other))
        return pairs

    everyone = ("zz", "x", "head")
    to_next = functools.partial(lax.ppermute, axis_name=everyone, perm=crossing(1))
    to_prev = functools.partial(lax.ppermute, axis_name=everyone, perm=crossing(-1))

    named = jnp.concatenate([key_lists, live_counts[:, None]], axis=1)
    ring = [named]
    for step in range(1, RING):
        ring.append(lax.ppermute(named, "x", [(i, (i + step) % RING) for i in range(RING)]))
    behind = jnp.mod(lax.axis_index("x") - jnp.arange(RING, dtype=jnp.int32), RING)
    named = jnp.take(jnp.stack(ring), behind, axis=0).reshape(GROUP, LISTED + 1)
    blocks = plane * GROUP + jnp.arange(GROUP, dtype=jnp.int32)
    window = blocks[:, None] - 1 + jnp.arange(WIN, dtype=jnp.int32)[None, :]
    window_ok = (window >= 0) & (window < planes * GROUP)
    listed_ok = jnp.arange(LISTED, dtype=jnp.int32)[None, :] < named[:, LISTED:]
    live = jnp.concatenate([window_ok, listed_ok], axis=1).astype(jnp.int32)
    places = jnp.concatenate([window, named[:, :LISTED]], axis=1) - plane * GROUP + HALO

    swap = functools.partial(lax.all_to_all, axis_name=team, split_axis=0, concat_axis=0, tiled=True)
    qd0, qd1 = send_queries(flip, qkv, grad_out)
    kv = swap(send_pairs(flip, qkv))
    kv, qd0 = lax.optimization_barrier((kv, qd0))
    halo0 = (to_next(kv[GROUP - HALO :, 0]), to_prev(kv[:HALO, 0]))
    qd0, halo0, qd1, edge1 = lax.optimization_barrier(
        (swap(qd0), halo0, qd1, (kv[GROUP - HALO :, 1], kv[:HALO, 1]))
    )
    halos = (halo0, (to_next(edge1[0]), to_prev(edge1[1])))
    qds = (qd0, swap(qd1))

    dq0, acc0, tobefore0, toafter0 = attention(0, places, live, kv, *halos[0], qds[0])
    back0 = (to_next(toafter0), to_prev(tobefore0))
    dq1, acc1, tobefore1, toafter1 = attention(1, places, live, kv, *halos[1], qds[1])
    back1 = (to_next(toafter1), to_prev(tobefore1))
    dq0 = swap(dq0)
    mid = swap(add_halo(acc0, *back0, dq1))
    held = join_early(flip, dq0, mid)
    dkv1 = swap(add_halo(acc1, *back1))
    return join_late(flip, dkv1, held)


def solution(mesh):
    shape = mesh.devices.shape
    inner = Mesh(mesh.devices.reshape(shape[0] // RING, RING, shape[1]), ("zz", "x", "head"))
    everyone = ("zz", "x", "head")
    placed = (P(everyone, None), P(everyone, None), P(("zz", "x"), None), P(("zz", "x")))
    return jax.shard_map(
        shards, mesh=inner, in_specs=placed, out_specs=P(everyone, None), check_vma=False
    )
```

```python
import functools

import jax
import jax.numpy as jnp
from jax import lax
from jax.experimental import pallas as pl
from jax.experimental.pallas import tpu as pltpu
from jax.sharding import Mesh
from jax.sharding import PartitionSpec as P

HD = 128
BLK = 128
TILES = 4
SPAN = 2
LISTED = 4
WIN = 3
RING = 4
GROUP = RING * TILES
HALO = SPAN * TILES
NAMED = 2
BACK = TILES + NAMED
EXT = GROUP + 2 * HALO
LOCAL = 2
SLOTS = WIN + LISTED
SIDES = 4
COLS = LOCAL * 3 * HD
LOG2E = 1.4426950408889634
F32 = jnp.float32
BF16 = jnp.bfloat16


VMEM = pl.BlockSpec(memory_space=pltpu.VMEM)
SMEM = pl.BlockSpec(memory_space=pltpu.SMEM)
HBM = pl.BlockSpec(memory_space=pl.ANY)


def run_all(pairs, sem):
    running = [pltpu.make_async_copy(s, d, sem.at[i]) for i, (s, d) in enumerate(pairs)]
    for c in running:
        c.start()
    for c in running:
        c.wait()


def columns(part, flip, head):
    pair = (part // 4) * 4 + jnp.bitwise_xor(part % 4, flip)
    at = pair * LOCAL + head
    return pl.multiple_of(at * 3 * HD, 3 * HD), pl.multiple_of(at * HD, HD)


def send_pairs_kernel(flip_ref, qkv_ref, kv_ref, sem):
    pairs = []
    for part in range(GROUP):
        for h in range(LOCAL):
            at, _ = columns(part, flip_ref[0], h)
            pairs.append((qkv_ref.at[:, pl.ds(at + HD, 2 * HD)], kv_ref.at[part, h]))
    run_all(pairs, sem)


def send_pairs(flip, qkv):
    return pl.pallas_call(
        send_pairs_kernel,
        out_shape=jax.ShapeDtypeStruct((GROUP, LOCAL, BLK, 2 * HD), BF16),
        in_specs=[SMEM, HBM],
        out_specs=VMEM,
        scratch_shapes=[pltpu.SemaphoreType.DMA((GROUP * LOCAL,))],
        compiler_params=pltpu.CompilerParams(vmem_limit_bytes=8 << 20),
        cost_estimate=pl.CostEstimate(flops=0, bytes_accessed=4 << 20, transcendentals=0),
    )(flip, qkv)


def send_queries_kernel(flip_ref, qkv_ref, grad_ref, qd_ref, sem):
    pairs = []
    for part in range(GROUP):
        for h in range(LOCAL):
            at, gat = columns(part, flip_ref[0], h)
            pairs.append((qkv_ref.at[:, pl.ds(at, HD)], qd_ref.at[part, h, :, pl.ds(0, HD)]))
            pairs.append((grad_ref.at[:, pl.ds(gat, HD)], qd_ref.at[part, h, :, pl.ds(HD, HD)]))
    run_all(pairs, sem)


def send_queries(flip, qkv, grad_out):
    return pl.pallas_call(
        send_queries_kernel,
        out_shape=jax.ShapeDtypeStruct((GROUP, LOCAL, BLK, 2 * HD), BF16),
        in_specs=[SMEM, HBM, HBM],
        out_specs=VMEM,
        scratch_shapes=[pltpu.SemaphoreType.DMA((GROUP * LOCAL * 2,))],
        compiler_params=pltpu.CompilerParams(vmem_limit_bytes=8 << 20),
        cost_estimate=pl.CostEstimate(flops=0, bytes_accessed=4 << 20, transcendentals=0),
    )(flip, qkv, grad_out)


def join_early_kernel(flip_ref, dq_ref, out_ref, sem):
    pairs = []
    for part in range(GROUP):
        for h in range(LOCAL):
            at, _ = columns(part, flip_ref[0], h)
            pairs.append((dq_ref.at[part, h], out_ref.at[:, pl.ds(at, HD)]))
    run_all(pairs, sem)


def join_early(flip, dq):
    return pl.pallas_call(
        join_early_kernel,
        out_shape=jax.ShapeDtypeStruct((BLK, GROUP * COLS), BF16),
        in_specs=[SMEM, VMEM],
        out_specs=HBM,
        scratch_shapes=[pltpu.SemaphoreType.DMA((GROUP * LOCAL,))],
        compiler_params=pltpu.CompilerParams(vmem_limit_bytes=8 << 20),
        cost_estimate=pl.CostEstimate(flops=0, bytes_accessed=2 << 20, transcendentals=0),
    )(flip, dq)


def join_late_kernel(flip_ref, dkv_ref, held_ref, out_ref, sem):
    pairs = []
    for part in range(GROUP):
        for h in range(LOCAL):
            at, _ = columns(part, flip_ref[0], h)
            pairs.append((dkv_ref.at[part, h], out_ref.at[:, pl.ds(at + HD, 2 * HD)]))
    run_all(pairs, sem)


def join_late(flip, dkv, held):
    return pl.pallas_call(
        join_late_kernel,
        out_shape=jax.ShapeDtypeStruct((BLK, GROUP * COLS), BF16),
        in_specs=[SMEM, VMEM, HBM],
        out_specs=HBM,
        scratch_shapes=[pltpu.SemaphoreType.DMA((GROUP * LOCAL,))],
        input_output_aliases={2: 0},
        compiler_params=pltpu.CompilerParams(vmem_limit_bytes=8 << 20),
        cost_estimate=pl.CostEstimate(flops=0, bytes_accessed=4 << 20, transcendentals=0),
    )(flip, dkv, held)


def add_kernel(ask_ref, own_ref, prev_ref, next_ref, out_ref):
    zero = jnp.zeros((), F32)
    for b in range(GROUP):
        for h in range(LOCAL):
            total = own_ref[b, h].astype(F32)
            if b < TILES:
                total = total + prev_ref[b, h].astype(F32)
            elif b < 2 * TILES:
                for i in range(NAMED):
                    hit = ask_ref[1, i] == b - TILES
                    total = total + jnp.where(hit, prev_ref[TILES + i, h].astype(F32), zero)
            elif b < GROUP - TILES:
                for i in range(NAMED):
                    hit = ask_ref[0, i] == b - (GROUP - 2 * TILES)
                    total = total + jnp.where(hit, next_ref[i, h].astype(F32), zero)
            else:
                total = total + next_ref[NAMED + b - (GROUP - TILES), h].astype(F32)
            out_ref[b, h] = total.astype(BF16)


def add_halo(ask, own, from_prev, from_next):
    return pl.pallas_call(
        add_kernel,
        out_shape=jax.ShapeDtypeStruct((GROUP, LOCAL, BLK, 2 * HD), BF16),
        in_specs=[SMEM] + [VMEM] * 3,
        out_specs=VMEM,
        compiler_params=pltpu.CompilerParams(vmem_limit_bytes=12 << 20),
        cost_estimate=pl.CostEstimate(flops=4 << 20, bytes_accessed=8 << 20, transcendentals=0),
    )(ask, own, from_prev, from_next)


def attention_kernel(
    place_ref,
    live_ref,
    want_ref,
    kv_ref,
    before_ref,
    after_ref,
    qd_ref,
    dq_ref,
    own_ref,
    tobefore_ref,
    toafter_ref,
    kv,
    qd,
    acc,
    mix,
    chosen,
    tall,
    low,
    dqs,
    outs,
    came,
    left,
):
    loads, stores = [], []
    for h in range(LOCAL):
        here = [
            (before_ref.at[:, h], kv.at[h, pl.ds(0, HALO)]),
            (kv_ref.at[:, h], kv.at[h, pl.ds(HALO, GROUP)]),
            (after_ref.at[:, h], kv.at[h, pl.ds(HALO + GROUP, HALO)]),
            (qd_ref.at[:, h], qd.at[h]),
        ]
        there = [
            (dqs.at[h], dq_ref.at[:, h]),
            (outs.at[h, pl.ds(TILES, TILES)], tobefore_ref.at[pl.ds(NAMED, TILES), h]),
            (outs.at[h, pl.ds(HALO, TILES)], toafter_ref.at[pl.ds(0, TILES), h]),
        ]
        for i in range(NAMED):
            there.append((outs.at[h, want_ref[0, i]], tobefore_ref.at[i, h]))
            there.append(
                (outs.at[h, HALO + TILES + want_ref[1, i]], toafter_ref.at[TILES + i, h])
            )
        loads.append([pltpu.make_async_copy(s, d, came.at[h, i]) for i, (s, d) in enumerate(here)])
        stores.append([pltpu.make_async_copy(s, d, left.at[h, i]) for i, (s, d) in enumerate(there)])
    for h in range(LOCAL):
        for c in loads[h]:
            c.start()
    acc[...] = jnp.zeros_like(acc)
    mix[...] = jnp.zeros_like(mix)
    for c in loads[0]:
        c.wait()
    scale = HD ** (-0.5)
    column = lax.broadcasted_iota(jnp.int32, (1, 1, 2 * HD), 2)
    factor = jnp.where(column < HD, scale, 1.0).astype(F32)

    def begin(head, block, side):
        mix[side, 0:BLK, 0:HD] = qd[head, block, :, 0:HD]
        mix[side, BLK : 2 * BLK, HD : 2 * HD] = qd[head, block, :, HD : 2 * HD]
        for j in range(SLOTS):
            chosen[side, j * BLK : (j + 1) * BLK] = kv[head, place_ref[block, j]]
        tall[side] = lax.dot_general(
            chosen[side], mix[side], (((1,), (1,)), ((), ())), preferred_element_type=F32
        )

    def middle(block, side):
        high = jnp.full((8, BLK), -3e38, F32)
        biases = [jnp.where(live_ref[block, j] > 0, 0.0, -1e30).astype(F32) for j in range(SLOTS)]
        for j in range(SLOTS):
            scores = tall[side, j * BLK : (j + 1) * BLK, 0:BLK] * (scale * LOG2E) + biases[j]
            high = jnp.maximum(high, jnp.max(scores.reshape(BLK // 8, 8, BLK), axis=0))
        top = jnp.max(high, axis=0, keepdims=True)
        total = jnp.zeros((8, BLK), F32)
        cross = jnp.zeros((8, BLK), F32)
        for j in range(SLOTS):
            rows = slice(j * BLK, (j + 1) * BLK)
            powers = jnp.exp2(tall[side, rows, 0:BLK] * (scale * LOG2E) + (biases[j] - top))
            tall[side, rows, 0:BLK] = powers
            total = total + jnp.sum(powers.reshape(BLK // 8, 8, BLK), axis=0)
            cross = cross + jnp.sum(
                (powers * tall[side, rows, BLK : 2 * BLK]).reshape(BLK // 8, 8, BLK), axis=0
            )
        inverse = 1.0 / jnp.sum(total, axis=0, keepdims=True)
        delta = jnp.sum(cross, axis=0, keepdims=True) * inverse
        for j in range(SLOTS):
            rows = slice(j * BLK, (j + 1) * BLK)
            soft = tall[side, rows, 0:BLK] * inverse
            low[side, rows, 0:BLK] = (soft * (tall[side, rows, BLK : 2 * BLK] - delta)).astype(BF16)
            low[side, rows, BLK : 2 * BLK] = soft.astype(BF16)

    def end(head, block, side):
        grad_query = lax.dot_general(
            low[side, :, 0:BLK],
            chosen[side, :, 0:HD],
            (((0,), (0,)), ((), ())),
            preferred_element_type=F32,
        )
        dqs[head, block] = (grad_query * scale).astype(BF16)
        back = lax.dot_general(
            low[side], mix[side], (((1,), (0,)), ((), ())), preferred_element_type=F32
        )
        for j in range(SLOTS):
            acc[head, place_ref[block, j]] += back[j * BLK : (j + 1) * BLK]

    def step(head):
        def run(i, _):
            for k in range(SIDES):
                begin(head, SIDES * i + k, k)
            for k in range(SIDES):
                middle(SIDES * i + k, k)
            for k in range(SIDES):
                end(head, SIDES * i + k, k)
            return 0

        return run

    for h in range(LOCAL):
        if h > 0:
            for c in loads[h]:
                c.wait()
        lax.fori_loop(0, GROUP // SIDES, step(h), 0)
        outs[h, 0:HALO] = (acc[h, 0:HALO] * factor).astype(BF16)
        outs[h, HALO:] = (acc[h, HALO + GROUP :] * factor).astype(BF16)
        for c in stores[h]:
            c.start()
        own_ref[:, h] = (acc[h, HALO : HALO + GROUP] * factor).astype(BF16)
    for h in range(LOCAL):
        for c in stores[h]:
            c.wait()


def attention(places, live, wants, kv, before, after, qd):
    return pl.pallas_call(
        attention_kernel,
        out_shape=[
            pltpu.HBM((GROUP, LOCAL, BLK, HD), BF16),
            jax.ShapeDtypeStruct((GROUP, LOCAL, BLK, 2 * HD), BF16),
            pltpu.HBM((BACK, LOCAL, BLK, 2 * HD), BF16),
            pltpu.HBM((BACK, LOCAL, BLK, 2 * HD), BF16),
        ],
        in_specs=[SMEM, SMEM, SMEM, HBM, HBM, HBM, HBM],
        out_specs=[HBM, VMEM, HBM, HBM],
        scratch_shapes=[
            pltpu.VMEM((LOCAL, EXT, BLK, 2 * HD), BF16),
            pltpu.VMEM((LOCAL, GROUP, BLK, 2 * HD), BF16),
            pltpu.VMEM((LOCAL, EXT, BLK, 2 * HD), F32),
            pltpu.VMEM((SIDES, 2 * BLK, 2 * HD), BF16),
            pltpu.VMEM((SIDES, SLOTS * BLK, 2 * HD), BF16),
            pltpu.VMEM((SIDES, SLOTS * BLK, 2 * BLK), F32),
            pltpu.VMEM((SIDES, SLOTS * BLK, 2 * BLK), BF16),
            pltpu.VMEM((LOCAL, GROUP, BLK, HD), BF16),
            pltpu.VMEM((LOCAL, 2 * HALO, BLK, 2 * HD), BF16),
            pltpu.SemaphoreType.DMA((LOCAL, 4)),
            pltpu.SemaphoreType.DMA((LOCAL, 3 + 2 * NAMED)),
        ],
        compiler_params=pltpu.CompilerParams(vmem_limit_bytes=30 << 20),
        cost_estimate=pl.CostEstimate(
            flops=4_800_000_000, bytes_accessed=16 << 20, transcendentals=4_000_000
        ),
    )(places, live, wants, *(pltpu.with_memory_space_constraint(x, pltpu.HBM) for x in (kv, before, after, qd)))


def shards(qkv, grad_out, key_lists, live_counts):
    planes = lax.axis_size("zz")
    plane = lax.axis_index("zz")
    team = ("x", "head")
    half = planes // 2
    flip = jnp.where(plane >= half, 2, 0).astype(jnp.int32).reshape(1)

    def crossing(step):
        pairs = []
        for p in range(planes):
            q = p + step
            if 0 <= q < planes:
                for r in range(RING):
                    for h in range(4):
                        other = h ^ 2 if (p >= half) != (q >= half) else h
                        pairs.append(((p * RING + r) * 4 + h, (q * RING + r) * 4 + other))
        return pairs

    everyone = ("zz", "x", "head")
    to_next = functools.partial(lax.ppermute, axis_name=everyone, perm=crossing(1))
    to_prev = functools.partial(lax.ppermute, axis_name=everyone, perm=crossing(-1))

    named = jnp.concatenate([key_lists, live_counts[:, None]], axis=1)
    ring = [named]
    for step in range(1, RING):
        ring.append(lax.ppermute(named, "x", [(i, (i + step) % RING) for i in range(RING)]))
    behind = jnp.mod(lax.axis_index("x") - jnp.arange(RING, dtype=jnp.int32), RING)
    named = jnp.take(jnp.stack(ring), behind, axis=0).reshape(GROUP, LISTED + 1)
    blocks = plane * GROUP + jnp.arange(GROUP, dtype=jnp.int32)
    window = blocks[:, None] - 1 + jnp.arange(WIN, dtype=jnp.int32)[None, :]
    window_ok = (window >= 0) & (window < planes * GROUP)
    listed_ok = jnp.arange(LISTED, dtype=jnp.int32)[None, :] < named[:, LISTED:]
    live = jnp.concatenate([window_ok, listed_ok], axis=1).astype(jnp.int32)
    places = jnp.concatenate([window, named[:, :LISTED]], axis=1) - plane * GROUP + HALO

    order = jnp.arange(TILES, dtype=jnp.int32)
    ends = jnp.stack([order, order + EXT - TILES])
    needed = jnp.any(places[None, :, :, None] == ends[:, None, None, :], axis=(1, 2))
    wants = jnp.stack(
        [
            jnp.min(jnp.where(needed, order, TILES - 1), axis=1),
            jnp.max(jnp.where(needed, order, 0), axis=1),
        ],
        axis=1,
    ).astype(jnp.int32)
    ask = jnp.stack([to_prev(wants[0]), to_next(wants[1])])
    once = jnp.where(ask[:, 1] == ask[:, 0], -1, ask[:, 1])
    ask = jnp.stack([ask[:, 0], once], axis=1)

    swap = functools.partial(lax.all_to_all, axis_name=team, split_axis=0, concat_axis=0, tiled=True)
    qd = send_queries(flip, qkv, grad_out)
    kv = swap(send_pairs(flip, qkv))
    kv, qd = lax.optimization_barrier((kv, qd))
    qd, ask = lax.optimization_barrier((swap(qd), ask))
    before, after = to_next(kv[GROUP - HALO :]), to_prev(kv[:HALO])
    dq, own, tobefore, toafter = attention(places, live, wants, kv, before, after, qd)
    from_prev, from_next = to_next(toafter), to_prev(tobefore)
    held = join_early(flip, swap(dq))
    dkv = swap(add_halo(ask, own, from_prev, from_next))
    return join_late(flip, dkv, held)


def solution(mesh):
    shape = mesh.devices.shape
    inner = Mesh(mesh.devices.reshape(shape[0] // RING, RING, shape[1]), ("zz", "x", "head"))
    everyone = ("zz", "x", "head")
    placed = (P(everyone, None), P(everyone, None), P(("zz", "x"), None), P(("zz", "x")))
    return jax.shard_map(
        shards, mesh=inner, in_specs=placed, out_specs=P(everyone, None), check_vma=False
    )
```

```python
import functools

import jax
import jax.numpy as jnp
from jax import lax
from jax.experimental import pallas as pl
from jax.experimental.pallas import tpu as pltpu
from jax.sharding import Mesh
from jax.sharding import PartitionSpec as P

HD = 128
BLK = 128
TILES = 4
SPAN = 2
LISTED = 4
WIN = 3
RING = 4
GROUP = RING * TILES
HALO = SPAN * TILES
EXT = GROUP + 2 * HALO
LOCAL = 2
SLOTS = WIN + LISTED
SIDES = 4
COLS = LOCAL * 3 * HD
LOG2E = 1.4426950408889634
F32 = jnp.float32
BF16 = jnp.bfloat16


VMEM = pl.BlockSpec(memory_space=pltpu.VMEM)
SMEM = pl.BlockSpec(memory_space=pltpu.SMEM)
HBM = pl.BlockSpec(memory_space=pl.ANY)


def run_all(pairs, sem):
    running = [pltpu.make_async_copy(s, d, sem.at[i]) for i, (s, d) in enumerate(pairs)]
    for c in running:
        c.start()
    for c in running:
        c.wait()


def columns(part, flip, head):
    pair = (part // 4) * 4 + jnp.bitwise_xor(part % 4, flip)
    at = pair * LOCAL + head
    return pl.multiple_of(at * 3 * HD, 3 * HD), pl.multiple_of(at * HD, HD)


def send_pairs_kernel(flip_ref, qkv_ref, kv_ref, sem):
    pairs = []
    for part in range(GROUP):
        for h in range(LOCAL):
            at, _ = columns(part, flip_ref[0], h)
            pairs.append((qkv_ref.at[:, pl.ds(at + HD, 2 * HD)], kv_ref.at[part, h]))
    run_all(pairs, sem)


def send_pairs(flip, qkv):
    return pl.pallas_call(
        send_pairs_kernel,
        out_shape=jax.ShapeDtypeStruct((GROUP, LOCAL, BLK, 2 * HD), BF16),
        in_specs=[SMEM, HBM],
        out_specs=VMEM,
        scratch_shapes=[pltpu.SemaphoreType.DMA((GROUP * LOCAL,))],
        compiler_params=pltpu.CompilerParams(vmem_limit_bytes=8 << 20),
        cost_estimate=pl.CostEstimate(flops=0, bytes_accessed=4 << 20, transcendentals=0),
    )(flip, qkv)


def send_queries_kernel(flip_ref, qkv_ref, grad_ref, qd_ref, sem):
    pairs = []
    for part in range(GROUP):
        for h in range(LOCAL):
            at, gat = columns(part, flip_ref[0], h)
            pairs.append((qkv_ref.at[:, pl.ds(at, HD)], qd_ref.at[part, h, :, pl.ds(0, HD)]))
            pairs.append((grad_ref.at[:, pl.ds(gat, HD)], qd_ref.at[part, h, :, pl.ds(HD, HD)]))
    run_all(pairs, sem)


def send_queries(flip, qkv, grad_out):
    return pl.pallas_call(
        send_queries_kernel,
        out_shape=jax.ShapeDtypeStruct((GROUP, LOCAL, BLK, 2 * HD), BF16),
        in_specs=[SMEM, HBM, HBM],
        out_specs=VMEM,
        scratch_shapes=[pltpu.SemaphoreType.DMA((GROUP * LOCAL * 2,))],
        compiler_params=pltpu.CompilerParams(vmem_limit_bytes=8 << 20),
        cost_estimate=pl.CostEstimate(flops=0, bytes_accessed=4 << 20, transcendentals=0),
    )(flip, qkv, grad_out)


def join_early_kernel(flip_ref, dq_ref, out_ref, sem):
    pairs = []
    for part in range(GROUP):
        for h in range(LOCAL):
            at, _ = columns(part, flip_ref[0], h)
            pairs.append((dq_ref.at[part, h], out_ref.at[:, pl.ds(at, HD)]))
    run_all(pairs, sem)


def join_early(flip, dq):
    return pl.pallas_call(
        join_early_kernel,
        out_shape=jax.ShapeDtypeStruct((BLK, GROUP * COLS), BF16),
        in_specs=[SMEM, VMEM],
        out_specs=HBM,
        scratch_shapes=[pltpu.SemaphoreType.DMA((GROUP * LOCAL,))],
        compiler_params=pltpu.CompilerParams(vmem_limit_bytes=8 << 20),
        cost_estimate=pl.CostEstimate(flops=0, bytes_accessed=2 << 20, transcendentals=0),
    )(flip, dq)


def join_late_kernel(flip_ref, dkv_ref, held_ref, out_ref, sem):
    pairs = []
    for part in range(GROUP):
        for h in range(LOCAL):
            at, _ = columns(part, flip_ref[0], h)
            pairs.append((dkv_ref.at[part, h], out_ref.at[:, pl.ds(at + HD, 2 * HD)]))
    run_all(pairs, sem)


def join_late(flip, dkv, held):
    return pl.pallas_call(
        join_late_kernel,
        out_shape=jax.ShapeDtypeStruct((BLK, GROUP * COLS), BF16),
        in_specs=[SMEM, VMEM, HBM],
        out_specs=HBM,
        scratch_shapes=[pltpu.SemaphoreType.DMA((GROUP * LOCAL,))],
        input_output_aliases={2: 0},
        compiler_params=pltpu.CompilerParams(vmem_limit_bytes=8 << 20),
        cost_estimate=pl.CostEstimate(flops=0, bytes_accessed=4 << 20, transcendentals=0),
    )(flip, dkv, held)


def add_kernel(own_ref, prev_ref, next_ref, out_ref):
    for b in range(GROUP):
        for h in range(LOCAL):
            more = prev_ref[b, h] if b < HALO else next_ref[b - HALO, h]
            out_ref[b, h] = (own_ref[b, h].astype(F32) + more.astype(F32)).astype(BF16)


def add_halo(own, from_prev, from_next):
    return pl.pallas_call(
        add_kernel,
        out_shape=jax.ShapeDtypeStruct((GROUP, LOCAL, BLK, 2 * HD), BF16),
        in_specs=[VMEM] * 3,
        out_specs=VMEM,
        compiler_params=pltpu.CompilerParams(vmem_limit_bytes=14 << 20),
        cost_estimate=pl.CostEstimate(flops=4 << 20, bytes_accessed=8 << 20, transcendentals=0),
    )(own, from_prev, from_next)


def attention_kernel(
    place_ref,
    live_ref,
    kv_ref,
    before_ref,
    after_ref,
    qd_ref,
    dq_ref,
    own_ref,
    tobefore_ref,
    toafter_ref,
    kv,
    qd,
    acc,
    mix,
    chosen,
    tall,
    low,
    dqs,
    outs,
    came,
    left,
):
    loads, stores = [], []
    for h in range(LOCAL):
        here = [
            (before_ref.at[:, h], kv.at[h, pl.ds(0, HALO)]),
            (kv_ref.at[:, h], kv.at[h, pl.ds(HALO, GROUP)]),
            (after_ref.at[:, h], kv.at[h, pl.ds(HALO + GROUP, HALO)]),
            (qd_ref.at[:, h], qd.at[h]),
        ]
        there = [
            (dqs.at[h], dq_ref.at[:, h]),
            (outs.at[h, pl.ds(0, HALO)], tobefore_ref.at[:, h]),
            (outs.at[h, pl.ds(HALO, HALO)], toafter_ref.at[:, h]),
        ]
        loads.append([pltpu.make_async_copy(s, d, came.at[h, i]) for i, (s, d) in enumerate(here)])
        stores.append([pltpu.make_async_copy(s, d, left.at[h, i]) for i, (s, d) in enumerate(there)])
    for h in range(LOCAL):
        for c in loads[h]:
            c.start()
    acc[...] = jnp.zeros_like(acc)
    mix[...] = jnp.zeros_like(mix)
    for c in loads[0]:
        c.wait()
    scale = HD ** (-0.5)
    column = lax.broadcasted_iota(jnp.int32, (1, 1, 2 * HD), 2)
    factor = jnp.where(column < HD, scale, 1.0).astype(F32)

    def begin(head, block, side):
        mix[side, 0:BLK, 0:HD] = qd[head, block, :, 0:HD]
        mix[side, BLK : 2 * BLK, HD : 2 * HD] = qd[head, block, :, HD : 2 * HD]
        for j in range(SLOTS):
            chosen[side, j * BLK : (j + 1) * BLK] = kv[head, place_ref[block, j]]
        tall[side] = lax.dot_general(
            chosen[side], mix[side], (((1,), (1,)), ((), ())), preferred_element_type=F32
        )

    def middle(block, side):
        high = jnp.full((8, BLK), -3e38, F32)
        biases = [jnp.where(live_ref[block, j] > 0, 0.0, -1e30).astype(F32) for j in range(SLOTS)]
        for j in range(SLOTS):
            scores = tall[side, j * BLK : (j + 1) * BLK, 0:BLK] * (scale * LOG2E) + biases[j]
            high = jnp.maximum(high, jnp.max(scores.reshape(BLK // 8, 8, BLK), axis=0))
        top = jnp.max(high, axis=0, keepdims=True)
        total = jnp.zeros((8, BLK), F32)
        cross = jnp.zeros((8, BLK), F32)
        for j in range(SLOTS):
            rows = slice(j * BLK, (j + 1) * BLK)
            powers = jnp.exp2(tall[side, rows, 0:BLK] * (scale * LOG2E) + (biases[j] - top))
            tall[side, rows, 0:BLK] = powers
            total = total + jnp.sum(powers.reshape(BLK // 8, 8, BLK), axis=0)
            cross = cross + jnp.sum(
                (powers * tall[side, rows, BLK : 2 * BLK]).reshape(BLK // 8, 8, BLK), axis=0
            )
        inverse = 1.0 / jnp.sum(total, axis=0, keepdims=True)
        delta = jnp.sum(cross, axis=0, keepdims=True) * inverse
        for j in range(SLOTS):
            rows = slice(j * BLK, (j + 1) * BLK)
            soft = tall[side, rows, 0:BLK] * inverse
            low[side, rows, 0:BLK] = (soft * (tall[side, rows, BLK : 2 * BLK] - delta)).astype(BF16)
            low[side, rows, BLK : 2 * BLK] = soft.astype(BF16)

    def end(head, block, side):
        grad_query = lax.dot_general(
            low[side, :, 0:BLK],
            chosen[side, :, 0:HD],
            (((0,), (0,)), ((), ())),
            preferred_element_type=F32,
        )
        dqs[head, block] = (grad_query * scale).astype(BF16)
        back = lax.dot_general(
            low[side], mix[side], (((1,), (0,)), ((), ())), preferred_element_type=F32
        )
        for j in range(SLOTS):
            acc[head, place_ref[block, j]] += back[j * BLK : (j + 1) * BLK]

    def step(head):
        def run(i, _):
            for k in range(SIDES):
                begin(head, SIDES * i + k, k)
            for k in range(SIDES):
                middle(SIDES * i + k, k)
            for k in range(SIDES):
                end(head, SIDES * i + k, k)
            return 0

        return run

    for h in range(LOCAL):
        if h > 0:
            for c in loads[h]:
                c.wait()
        lax.fori_loop(0, GROUP // SIDES, step(h), 0)
        outs[h, 0:HALO] = (acc[h, 0:HALO] * factor).astype(BF16)
        outs[h, HALO : 2 * HALO] = (acc[h, HALO + GROUP : EXT] * factor).astype(BF16)
        for c in stores[h]:
            c.start()
        own_ref[:, h] = (acc[h, HALO : HALO + GROUP] * factor).astype(BF16)
    for h in range(LOCAL):
        for c in stores[h]:
            c.wait()


def attention(places, live, kv, before, after, qd):
    return pl.pallas_call(
        attention_kernel,
        out_shape=[
            pltpu.HBM((GROUP, LOCAL, BLK, HD), BF16),
            jax.ShapeDtypeStruct((GROUP, LOCAL, BLK, 2 * HD), BF16),
            pltpu.HBM((HALO, LOCAL, BLK, 2 * HD), BF16),
            pltpu.HBM((HALO, LOCAL, BLK, 2 * HD), BF16),
        ],
        in_specs=[SMEM, SMEM, HBM, HBM, HBM, HBM],
        out_specs=[HBM, VMEM, HBM, HBM],
        scratch_shapes=[
            pltpu.VMEM((LOCAL, EXT, BLK, 2 * HD), BF16),
            pltpu.VMEM((LOCAL, GROUP, BLK, 2 * HD), BF16),
            pltpu.VMEM((LOCAL, EXT, BLK, 2 * HD), F32),
            pltpu.VMEM((SIDES, 2 * BLK, 2 * HD), BF16),
            pltpu.VMEM((SIDES, SLOTS * BLK, 2 * HD), BF16),
            pltpu.VMEM((SIDES, SLOTS * BLK, 2 * BLK), F32),
            pltpu.VMEM((SIDES, SLOTS * BLK, 2 * BLK), BF16),
            pltpu.VMEM((LOCAL, GROUP, BLK, HD), BF16),
            pltpu.VMEM((LOCAL, 2 * HALO, BLK, 2 * HD), BF16),
            pltpu.SemaphoreType.DMA((LOCAL, 4)),
            pltpu.SemaphoreType.DMA((LOCAL, 3)),
        ],
        compiler_params=pltpu.CompilerParams(vmem_limit_bytes=30 << 20),
        cost_estimate=pl.CostEstimate(
            flops=4_800_000_000, bytes_accessed=16 << 20, transcendentals=4_000_000
        ),
    )(
        places,
        live,
        *(pltpu.with_memory_space_constraint(x, pltpu.HBM) for x in (kv, before, after, qd)),
    )


def shards(qkv, grad_out, key_lists, live_counts):
    planes = lax.axis_size("zz")
    plane = lax.axis_index("zz")
    team = ("x", "head")
    half = planes // 2
    flip = jnp.where(plane >= half, 2, 0).astype(jnp.int32).reshape(1)

    def crossing(step):
        pairs = []
        for p in range(planes):
            q = p + step
            if 0 <= q < planes:
                for r in range(RING):
                    for h in range(4):
                        other = h ^ 2 if (p >= half) != (q >= half) else h
                        pairs.append(((p * RING + r) * 4 + h, (q * RING + r) * 4 + other))
        return pairs

    everyone = ("zz", "x", "head")
    to_next = functools.partial(lax.ppermute, axis_name=everyone, perm=crossing(1))
    to_prev = functools.partial(lax.ppermute, axis_name=everyone, perm=crossing(-1))

    named = jnp.concatenate([key_lists, live_counts[:, None]], axis=1)
    ring = [named]
    for step in range(1, RING):
        ring.append(lax.ppermute(named, "x", [(i, (i + step) % RING) for i in range(RING)]))
    behind = jnp.mod(lax.axis_index("x") - jnp.arange(RING, dtype=jnp.int32), RING)
    named = jnp.take(jnp.stack(ring), behind, axis=0).reshape(GROUP, LISTED + 1)
    blocks = plane * GROUP + jnp.arange(GROUP, dtype=jnp.int32)
    window = blocks[:, None] - 1 + jnp.arange(WIN, dtype=jnp.int32)[None, :]
    window_ok = (window >= 0) & (window < planes * GROUP)
    listed_ok = jnp.arange(LISTED, dtype=jnp.int32)[None, :] < named[:, LISTED:]
    live = jnp.concatenate([window_ok, listed_ok], axis=1).astype(jnp.int32)
    places = jnp.concatenate([window, named[:, :LISTED]], axis=1) - plane * GROUP + HALO

    swap = functools.partial(lax.all_to_all, axis_name=team, split_axis=0, concat_axis=0, tiled=True)
    qd = send_queries(flip, qkv, grad_out)
    kv = swap(send_pairs(flip, qkv))
    kv, qd = lax.optimization_barrier((kv, qd))
    qd = swap(qd)
    before, after = to_next(kv[GROUP - HALO :]), to_prev(kv[:HALO])
    dq, own, tobefore, toafter = attention(places, live, kv, before, after, qd)
    from_prev, from_next = to_next(toafter), to_prev(tobefore)
    held = join_early(flip, swap(dq))
    dkv = swap(add_halo(own, from_prev, from_next))
    return join_late(flip, dkv, held)


def solution(mesh):
    shape = mesh.devices.shape
    inner = Mesh(mesh.devices.reshape(shape[0] // RING, RING, shape[1]), ("zz", "x", "head"))
    everyone = ("zz", "x", "head")
    placed = (P(everyone, None), P(everyone, None), P(("zz", "x"), None), P(("zz", "x")))
    return jax.shard_map(
        shards, mesh=inner, in_specs=placed, out_specs=P(everyone, None), check_vma=False
    )
```
